32 devices in a mesh: ens: 2 (over x), region: 16 (over z, y, core).
Axes of the slice: x: 2, y: 2, z: 4, core: 2. Of those that a mesh axis runs over, the one named last changes fastest.
Arguments:
- node_latent: bfloat16 [16384, 512], P(('ens', 'region')), parts along dimension 0, may hold values from -6 to 6
- grid_latent: bfloat16 [16384, 512], P(('ens', 'region')), parts along dimension 0, may hold values from -6 to 6
- fine_edge_sender: int32 [65536], P(('ens', 'region')), parts along dimension 0, may hold values from 0 to 8191, as said below
- short_recv: int32 [65536], P(('ens', 'region')), parts along dimension 0, may hold values from 0 to 511
- short_geo: float32 [4, 65536], P(None, ('ens', 'region')), parts along dimension 1, may hold values from -6 to 6
- long_send: int32 [16384], P(('ens', 'region')), parts along dimension 0, may hold values from -1 to 8191, as said below
- long_recv: int32 [16384], P(('ens', 'region')), parts along dimension 0, may hold values from 0 to 511
- long_geo: float32 [4, 16384], P(None, ('ens', 'region')), parts along dimension 1, may hold values from -6 to 6
- dec_send: int32 [3, 16384], P(None, ('ens', 'region')), parts along dimension 1, may hold values from 0 to 8191, as said below
- dec_geo: float32 [4, 3, 16384], P(None, None, ('ens', 'region')), parts along dimension 2, may hold values from -6 to 6
- w_send: bfloat16 [512, 512], replicated, may hold values from -0.25 to 0.25
- w_recv: bfloat16 [512, 512], replicated, may hold values from -0.25 to 0.25
- w_edge_geo: float32 [4, 512], replicated, may hold values from -3 to 3
- w_message: bfloat16 [512, 512], replicated, may hold values from -0.25 to 0.25
- w_node_self: bfloat16 [512, 512], replicated, may hold values from -0.25 to 0.25
- w_node_agg: bfloat16 [512, 512], replicated, may hold values from -0.25 to 0.25
- w_node_out: bfloat16 [512, 512], replicated, may hold values from -0.25 to 0.25
- w_dec_send: bfloat16 [512, 512], replicated, may hold values from -0.25 to 0.25
- w_dec_grid: bfloat16 [512, 512], replicated, may hold values from -0.25 to 0.25
- w_dec_geo: float32 [4, 512], replicated, may hold values from -3 to 3
- decoding_link_final_matrix: bfloat16 [512, 512], replicated, may hold values from -0.25 to 0.25
- w_grid_agg: bfloat16 [512, 512], replicated, may hold values from -0.25 to 0.25
- w_grid_self: bfloat16 [512, 512], replicated, may hold values from -0.25 to 0.25
- final_projection_matrix: bfloat16 [100, 512], replicated, may hold values from -0.25 to 0.25
Outputs:
- refreshed_mesh_latents: bfloat16 [16384, 512], P(('ens', 'region')), parts along dimension 0
- predicted_fields: bfloat16 [100, 16384], P(None, ('ens', 'region')), parts along dimension 1
The draws below stay inside these ranges and needn't reach their ends.
There are 2 independent parts, one for each index of `ens`. The reference program is written for one: setup_inputs(seed, part) draws one part's arguments, and reference() takes and returns one part's arrays. A program takes and returns all parts, laid end to end along the dimension named above; an argument that names none is the same for every part. Nothing has to cross between parts.
Inputs may be any that keep to these rules, and one draw needn't show every extreme that they name: `fine_edge_sender`: A fine edge held by region d has its sender in region d, among the last 64 nodes of region d - 1, or among the first 64 nodes of region d + 1; node 448 of region d - 1 (the first of its last 64) and node 63 of region d + 1 are used where those regions exist. `long_send`: slot d * 512 + o * 32 + j, unless -1, names one of the first 64 nodes of region o; in every region one other region's 32 slots are all filled. `dec_send`: the senders of a grid point of band d lie in region d, among the last 64 nodes of region d - 1, or among the first 64 nodes of region d + 1; node 448 of region d - 1 (the first of its last 64) and node 63 of region d + 1 are used where those regions exist.
All inputs are finite; a program needn't handle non-finite values.
Results may differ from the reference program's by a relative error of at most 0.013.
Values may be sent and summed in bfloat16 or wider, within the bound.
A program may use at most 128 MiB of HBM per device.

```python
import jax
import jax.numpy as jnp
from jax import lax

H = 512
C_OUT = 100
GEO = 4
MESH_DEV = 512
G_DEV = 512
LONG_DEV = 512
BORDER = 64
SHORT_DEV = 2048
COARSE_DEV = 64
SLOT = 32
MESH_NODES = 8192
GRID = 8192
N_REGION = 16


def rim_draw(key, processor_part, within):
    first, second, third = jax.random.split(key, 3)
    extent = processor_part.shape
    kind = jax.random.randint(first, extent, 0, 6)
    kind = jnp.where(within == 0, 0, jnp.where(within == 1, 1, kind))
    local = jax.random.randint(second, extent, 0, MESH_DEV)
    depth = jax.random.randint(third, extent, 0, BORDER)
    depth = jnp.where(within == 0, 0, jnp.where(within == 1, BORDER - 1, depth))
    lower = (processor_part - 1) * MESH_DEV + MESH_DEV - BORDER + depth
    upper = (processor_part + 1) * MESH_DEV + depth
    own_node = processor_part * MESH_DEV + local
    picked = jnp.where((kind == 0) & (processor_part > 0), lower, jnp.where((kind == 1) & (processor_part < N_REGION - 1), upper, own_node))
    return picked.astype(jnp.int32)


def draw_fine_edge_sender(key, part):
    position = jnp.arange(N_REGION * SHORT_DEV, dtype=jnp.int32)
    return rim_draw(jax.random.fold_in(key, 11), position // SHORT_DEV, position % SHORT_DEV)


def draw_dec_send(key, part):
    points = jnp.arange(N_REGION * G_DEV, dtype=jnp.int32)
    vertex = jnp.arange(3, dtype=jnp.int32)[:, None]
    processor_part = jnp.broadcast_to((points // G_DEV)[None, :], (3, N_REGION * G_DEV))
    within = (points % G_DEV)[None, :] * 3 + vertex
    return rim_draw(jax.random.fold_in(key, 23), processor_part, within)


def draw_long_send(key, part):
    first, second, third = jax.random.split(jax.random.fold_in(key, 37), 3)
    position = jnp.arange(N_REGION * LONG_DEV, dtype=jnp.int32)
    processor_part = position // LONG_DEV
    within = position % LONG_DEV
    owner = within // SLOT
    column = within % SLOT
    levels = jax.random.randint(first, (N_REGION,), 20, 101)
    live = jax.random.randint(second, position.shape, 0, 100) < levels[processor_part]
    filled = owner == (processor_part * 7 + 3) % N_REGION
    live = live | filled
    local = jax.random.randint(third, position.shape, 0, COARSE_DEV)
    local = jnp.where(filled & (column == 0), COARSE_DEV - 1, local)
    return jnp.where(live, owner * MESH_DEV + local, -1).astype(jnp.int32)


def place_ends(result, rng, smallest, top_value):
    index_at = [jax.random.randint(jax.random.fold_in(rng, axis), (), 0, length) for axis, length in enumerate(result.shape)]
    main_axis = result.shape.index(max(result.shape))
    next_to = index_at[:main_axis] + [(index_at[main_axis] + 1) % result.shape[main_axis]] + index_at[main_axis + 1:]
    return result.at[tuple(index_at)].set(smallest).at[tuple(next_to)].set(top_value)


def steps_of(stream_key, shape, shards, low, high):
    gain = 1.0
    for dim, shards_of in shards:
        draws = jax.random.uniform(jax.random.fold_in(jax.random.fold_in(stream_key, 6), dim), (shards_of,), jnp.float32, low / len(shards), high / len(shards))
        gain = gain * jnp.repeat(jnp.exp(draws), shape[dim] // shards_of).reshape((-1,) + (1,) * (len(shape) - 1 - dim))
    return gain


def noise(key, shape, deviation, bound, pieces=(), kind=jnp.bfloat16):
    values = jax.random.normal(key, shape, jnp.float32) * deviation
    if len(pieces) > 0:
        values = steps_of(key, shape, pieces, -0.22, 0.18) * values
    return jnp.clip(values, min=-bound, max=bound).astype(kind)


def setup_inputs(seed: int = 0, part: int = 0) -> dict:
    key_of = jax.random.split(jax.random.key(seed), 25)
    part_keys = jax.random.split(jax.random.fold_in(key_of[24], part), 25)
    node_latent = noise(part_keys[0], (MESH_NODES, H), 1.0, 6.0, ((0, 16),))
    grid_latent = noise(part_keys[1], (GRID, H), 1.0, 6.0, ((0, 16),))
    fine_edge_sender = draw_fine_edge_sender(jax.random.fold_in(jax.random.fold_in(key_of[24], part), 71), part)
    short_recv = place_ends(jax.random.randint(part_keys[3], (N_REGION * SHORT_DEV,), 0, MESH_DEV), jax.random.fold_in(part_keys[3], 1), 0, MESH_DEV - 1).astype(jnp.int32)
    short_geo = noise(part_keys[4], (GEO, N_REGION * SHORT_DEV), 1.0, 6.0, ((1, 16),), jnp.float32)
    long_send = draw_long_send(jax.random.fold_in(jax.random.fold_in(key_of[24], part), 71), part)
    long_recv = place_ends(jax.random.randint(part_keys[6], (N_REGION * LONG_DEV,), 0, MESH_DEV), jax.random.fold_in(part_keys[6], 1), 0, MESH_DEV - 1).astype(jnp.int32)
    long_geo = noise(part_keys[7], (GEO, N_REGION * LONG_DEV), 1.0, 6.0, ((1, 16),), jnp.float32)
    dec_send = draw_dec_send(jax.random.fold_in(jax.random.fold_in(key_of[24], part), 71), part)
    dec_geo = noise(part_keys[9], (GEO, 3, GRID), 1.0, 6.0, ((2, 16),), jnp.float32)
    w_send = noise(key_of[10], (H, H), H ** -0.5, 0.25)
    w_recv = noise(key_of[11], (H, H), H ** -0.5, 0.25)
    w_edge_geo = noise(key_of[12], (GEO, H), GEO ** -0.5, 3.0, (), jnp.float32)
    w_message = noise(key_of[13], (H, H), H ** -0.5, 0.25)
    w_node_self = noise(key_of[14], (H, H), H ** -0.5, 0.25)
    w_node_agg = noise(key_of[15], (H, H), H ** -0.5, 0.25)
    w_node_out = noise(key_of[16], (H, H), H ** -0.5, 0.25)
    w_dec_send = noise(key_of[17], (H, H), H ** -0.5, 0.25)
    w_dec_grid = noise(key_of[18], (H, H), H ** -0.5, 0.25)
    w_dec_geo = noise(key_of[19], (GEO, H), GEO ** -0.5, 3.0, (), jnp.float32)
    decoding_link_final_matrix = noise(key_of[20], (H, H), H ** -0.5, 0.25)
    w_grid_agg = noise(key_of[21], (H, H), H ** -0.5, 0.25)
    w_grid_self = noise(key_of[22], (H, H), H ** -0.5, 0.25)
    final_projection_matrix = noise(key_of[23], (C_OUT, H), H ** -0.5, 0.25)
    return {"node_latent": node_latent, "grid_latent": grid_latent, "fine_edge_sender": fine_edge_sender, "short_recv": short_recv, "short_geo": short_geo, "long_send": long_send, "long_recv": long_recv, "long_geo": long_geo, "dec_send": dec_send, "dec_geo": dec_geo, "w_send": w_send, "w_recv": w_recv, "w_edge_geo": w_edge_geo, "w_message": w_message, "w_node_self": w_node_self, "w_node_agg": w_node_agg, "w_node_out": w_node_out, "w_dec_send": w_dec_send, "w_dec_grid": w_dec_grid, "w_dec_geo": w_dec_geo, "decoding_link_final_matrix": decoding_link_final_matrix, "w_grid_agg": w_grid_agg, "w_grid_self": w_grid_self, "final_projection_matrix": final_projection_matrix}


def product(left, right):
    return jnp.dot(left, right, preferred_element_type=jnp.float32)

def geometry(feature_vectors, learned_factor):
    return lax.dot_general(feature_vectors, learned_factor, (((0,), (0,)), ((), ())), precision=lax.Precision.HIGHEST)

def normalize(values):
    middle_point = values - lax.optimization_barrier(jnp.mean(values, axis=-1, keepdims=True))
    spread = lax.optimization_barrier(jnp.mean(middle_point * middle_point, axis=-1, keepdims=True))
    return middle_point * lax.rsqrt(spread + 1e-05)

def messages(edge_pre, w_message):
    edge_hidden = jax.nn.silu(edge_pre).astype(jnp.bfloat16)
    return normalize(product(edge_hidden, w_message))

def reference(node_latent, grid_latent, fine_edge_sender, short_recv, short_geo, long_send, long_recv, long_geo, dec_send, dec_geo, w_send, w_recv, w_edge_geo, w_message, w_node_self, w_node_agg, w_node_out, w_dec_send, w_dec_grid, w_dec_geo, decoding_link_final_matrix, w_grid_agg, w_grid_self, final_projection_matrix):
    total_nodes = node_latent.shape[0]
    channel_count = node_latent.shape[1]
    send_proj = product(node_latent, w_send)
    recv_proj = product(node_latent, w_recv)
    fine_target = short_recv + jnp.arange(N_REGION * SHORT_DEV, dtype=jnp.int32) // SHORT_DEV * MESH_DEV
    fine_pre = send_proj[fine_edge_sender] + recv_proj[fine_target] + geometry(short_geo, w_edge_geo)
    fine_msg = messages(fine_pre, w_message)
    present = long_send >= 0
    clipped = jnp.maximum(long_send, 0)
    far_target = long_recv + jnp.arange(N_REGION * LONG_DEV, dtype=jnp.int32) // LONG_DEV * MESH_DEV
    far_pre = send_proj[clipped] + recv_proj[far_target] + geometry(long_geo, w_edge_geo)
    far_msg = messages(far_pre, w_message) * present[:, None].astype(fine_msg.dtype)
    aggregate = jnp.zeros((total_nodes, channel_count), fine_msg.dtype).at[fine_target].add(fine_msg).at[far_target].add(far_msg)
    node_hidden = jax.nn.silu(product(node_latent, w_node_self) + product(aggregate.astype(jnp.bfloat16), w_node_agg)).astype(jnp.bfloat16)
    refreshed_mesh_latents = (node_latent.astype(jnp.float32) + product(node_hidden, w_node_out)).astype(jnp.bfloat16)
    dec_proj = product(refreshed_mesh_latents, w_dec_send)
    grid_proj = product(grid_latent, w_dec_grid)
    grid_sum = jnp.zeros(grid_proj.shape, grid_proj.dtype)
    for vertex in range(3):
        dec_pre = dec_proj[dec_send[vertex]] + grid_proj + geometry(dec_geo[:, vertex, :], w_dec_geo)
        grid_sum = grid_sum + messages(dec_pre, decoding_link_final_matrix)
    grid_agg = grid_sum.astype(jnp.bfloat16)
    latitude_site_latent_matrix = jax.nn.silu(product(grid_agg, w_grid_agg) + product(grid_latent, w_grid_self)).astype(jnp.bfloat16)
    predicted_fields = lax.dot_general(final_projection_matrix, latitude_site_latent_matrix, (((1,), (1,)), ((), ())), preferred_element_type=jnp.float32).astype(jnp.bfloat16)
    return (refreshed_mesh_latents, predicted_fields)
```

```python
import functools

import jax
import jax.numpy as jnp
from jax import lax
from jax.experimental import pallas as pl
from jax.experimental.pallas import tpu as pltpu
from jax.sharding import PartitionSpec as P

BORDER = 64
COARSE = 64
TAIL = 128
LANES = 128
CHUNK = 512
F32 = jnp.float32
BF16 = jnp.bfloat16
MESH = pl.DeviceIdType.MESH


def dot(left, right):
    return jnp.dot(left, right, preferred_element_type=F32)


def silu(value):
    half = 0.5 * value
    return half + half * jnp.tanh(half)


def normalize(values):
    width = 1.0 / values.shape[-1]
    centred = values - jnp.sum(values, axis=-1, keepdims=True) * width
    spread = jnp.sum(centred * centred, axis=-1, keepdims=True) * width
    return centred * lax.rsqrt(spread + 1e-5)


def one_hot(place, count):
    lanes = lax.broadcasted_iota(jnp.int32, (place.shape[0], count), 1)
    return jnp.where(lanes == place, 1.0, 0.0).astype(BF16)


def one_hot_rows(place, count):
    rows = lax.broadcasted_iota(jnp.int32, (count, place.shape[1]), 0)
    return jnp.where(rows == place, 1.0, 0.0).astype(BF16)


def turn(slab):
    parts = []
    for start in range(0, slab.shape[1], LANES):
        piece = slab[:, start : start + LANES]
        full = jnp.concatenate([piece, jnp.zeros((LANES - 16, LANES), F32)], axis=0)
        parts.append(full.T)
    return jnp.concatenate(parts, axis=0)


def put_geometry(slab, geo):
    high = geo.astype(BF16).astype(F32)
    slab[4:8, :] = high
    slab[8:12, :] = geo - high
    slab[12:16, :] = high


def put_tail(table, start, w_geo):
    high = w_geo.astype(BF16).astype(F32)
    width = w_geo.shape[1]
    rows = jnp.concatenate(
        [jnp.zeros((4, width), F32), high, high, w_geo - high, jnp.zeros((TAIL - 16, width), F32)],
        axis=0,
    )
    table[start : start + TAIL, :] = rows.astype(BF16)


def kernel(
    regions,
    node,
    grid_hbm,
    fine_send,
    fine_recv,
    fine_geo,
    long_send,
    long_recv,
    long_geo,
    dec_send,
    dec_geo,
    w_send,
    w_recv,
    w_edge_geo,
    w_dec_geo,
    w_message_hbm,
    w_node_self_hbm,
    w_node_agg_hbm,
    w_node_out_hbm,
    w_dec_send_hbm,
    w_dec_grid_hbm,
    w_dec_final_hbm,
    w_grid_agg_hbm,
    w_grid_self_hbm,
    w_final_hbm,
    out_mesh,
    out_fields,
    grid,
    w_message,
    w_node_self,
    w_node_agg,
    w_node_out,
    w_dec_send,
    w_dec_grid,
    w_dec_final,
    w_grid_agg,
    w_grid_self,
    w_final,
    load_sem,
    edge_in,
    ends_out,
    ends_in,
    border_send,
    border_recv,
    coarse,
    z_send,
    z_recv,
    y_send,
    y_recv,
    c_send,
    c_recv,
    table,
    coarse_table,
    dec_table,
    slab_fine,
    slab_long,
    slab_dec,
    total,
    self_part,
    grid_part,
    grid_own,
):
    nodes, width = node.shape
    edges = slab_fine.shape[1]
    slots = slab_long.shape[1]
    points = slab_dec.shape[2]
    span = nodes + 2 * BORDER
    ens = lax.axis_index("ens")
    me = lax.axis_index("region")
    line = regions // 4
    spot = me // 4
    lane = me % 4
    twin = me + 1 - 2 * (me % 2)
    side = lane % 4
    across = me + 2 - 4 * (side // 2)

    loads = [
        (grid_hbm, grid),
        (w_message_hbm, w_message),
        (w_node_self_hbm, w_node_self),
        (w_node_agg_hbm, w_node_agg),
        (w_node_out_hbm, w_node_out),
        (w_dec_send_hbm, w_dec_send),
        (w_dec_grid_hbm, w_dec_grid),
        (w_dec_final_hbm, w_dec_final),
        (w_grid_agg_hbm, w_grid_agg),
        (w_grid_self_hbm, w_grid_self),
        (w_final_hbm, w_final),
    ]

    def load(number):
        return pltpu.make_async_copy(*loads[number], load_sem.at[number])

    for number in (1, 2, 0, 3, 4, 5, 6, 7, 8, 9, 10):
        load(number).start()

    has_left, has_right = me > 0, me < regions - 1
    has_back, has_next = spot > 0, spot < line - 1

    barrier = pltpu.get_barrier_semaphore()

    def greet(other):
        pl.semaphore_signal(barrier, inc=1, device_id=(ens, other), device_id_type=MESH)

    greet(across)
    for present, other in (
        (has_left, me - 1),
        (has_right, me + 1),
        (has_back, me - 4),
        (has_next, me + 4),
    ):
        pl.when(present)(functools.partial(greet, other))
    coarse[me] = node[:COARSE, :]
    count = 1
    for present in (has_left, has_right, has_back, has_next):
        count = count + present.astype(jnp.int32)
    pl.semaphore_wait(barrier, count)

    def remote(src, dst, send, recv, other):
        return pltpu.make_async_remote_copy(
            src_ref=src,
            dst_ref=dst,
            send_sem=send,
            recv_sem=recv,
            device_id=(ens, other),
            device_id_type=MESH,
        )

    def border_up(src, phase, into):
        return remote(
            src, into.at[0], border_send.at[phase, 0], border_recv.at[phase, 0], me + 1
        )

    def border_down(src, phase, into):
        return remote(
            src, into.at[1], border_send.at[phase, 1], border_recv.at[phase, 1], me - 1
        )

    def exchange(first, last, phase, into):
        pl.when(has_right)(lambda: border_up(last, phase, into).start())
        pl.when(has_left)(lambda: border_down(first, phase, into).start())

        @pl.when(jnp.logical_not(has_left))
        def _():
            into[0] = jnp.zeros((BORDER, width), BF16)

        @pl.when(jnp.logical_not(has_right))
        def _():
            into[1] = jnp.zeros((BORDER, width), BF16)

    def settle(first, last, phase, into):
        @pl.when(has_right)
        def _():
            border_up(last, phase, into).wait_send()
            border_down(first, phase, into).wait_recv()

        @pl.when(has_left)
        def _():
            border_down(first, phase, into).wait_send()
            border_up(last, phase, into).wait_recv()

    node_first, node_last = node.at[pl.ds(0, BORDER)], node.at[pl.ds(nodes - BORDER, BORDER)]
    exchange(node_first, node_last, 0, edge_in)

    def z_copy(way, step, place):
        block = coarse.at[place * 4 + lane]
        other = me + 4 - 8 * way
        return remote(block, block, z_send.at[way, step], z_recv.at[way, step], other)

    def y_copy(place):
        block = coarse.at[place * 4 + lane]
        return remote(block, block, y_send.at[place], y_recv.at[place], across)

    def c_copy(half, place):
        block = coarse.at[place * 4 + (lane + 2 * half) % 4]
        return remote(block, block, c_send.at[half, place], c_recv.at[half, place], twin)

    def spread(place):
        y_copy(place).start()
        c_copy(0, place).start()

    def step_z(step):
        for way in range(2):
            place = spot - step if way == 0 else spot + step
            held = (place >= 0) & (place < line)

            @pl.when(held)
            def _():
                if step > 0:
                    z_copy(way, step - 1, place).wait_recv()
                if step < line - 1:
                    onward = has_next if way == 0 else has_back
                    pl.when(onward)(lambda: z_copy(way, step, place).start())
                if step > 0 or way == 0:
                    spread(place)

    def step_y():
        for place in range(line):
            y_copy(place).wait_recv()
            c_copy(1, place).start()

    def step_end():
        for place in range(line):
            for half in range(2):
                c_copy(half, place).wait()
            y_copy(place).wait_send()
        for step in range(line - 1):
            for way in range(2):
                place = spot - step if way == 0 else spot + step
                onward = has_next if way == 0 else has_back
                held = (place >= 0) & (place < line) & onward
                pl.when(held)(lambda: z_copy(way, step, place).wait_send())

    step_z(0)

    own = node[...]
    table[BORDER : BORDER + nodes, :] = dot(own, w_send[...]).astype(BF16)
    table[span : span + nodes, :] = dot(own, w_recv[...]).astype(BF16)
    put_tail(table, span + nodes, w_edge_geo[...])
    put_tail(dec_table, span, w_dec_geo[...])
    offset = me * nodes - BORDER
    for slab, geo in ((slab_fine, fine_geo[...]), (slab_long, long_geo[...])):
        put_geometry(slab, geo)
        slab[2:4, :] = jnp.zeros((2, geo.shape[1]), F32)
    for row in range(edges // LANES):
        at = pl.ds(row * LANES, LANES)
        slab_fine[0:1, at] = (fine_send[row : row + 1, :] - offset).astype(F32)
        slab_fine[1:2, at] = fine_recv[row : row + 1, :].astype(F32)
    per_owner = slots // regions
    group = max(per_owner, slots // 2)
    owners = group // per_owner
    for row in range(slots // LANES):
        at = pl.ds(row * LANES, LANES)
        slot = lax.broadcasted_iota(jnp.int32, (1, LANES), 1) + row * LANES
        owner = slot // per_owner
        sender = long_send[row : row + 1, :]
        base = (row * LANES // group) * owners
        within = sender - owner * nodes + (owner - base) * COARSE
        full = sender >= 0
        slab_long[0:1, at] = jnp.where(full, within, -1).astype(F32)
        slab_long[1:2, at] = jnp.where(full, long_recv[row : row + 1, :], -1).astype(F32)
    for k in range(3):
        slab_dec[k, 0:1, :] = (dec_send[k : k + 1, :] - offset).astype(F32)
        slab_dec[k, 1:4, :] = jnp.zeros((3, points), F32)
        for i in range(4):
            geo = dec_geo[i, k : k + 1, :]
            high = geo.astype(BF16).astype(F32)
            slab_dec[k, 4 + i : 5 + i, :] = high
            slab_dec[k, 8 + i : 9 + i, :] = geo - high
            slab_dec[k, 12 + i : 13 + i, :] = high
    total[...] = jnp.zeros(total.shape, F32)
    load(2).wait()
    self_part[...] = dot(own, w_node_self[...])
    load(1).wait()

    settle(node_first, node_last, 0, edge_in)
    border = jnp.concatenate([edge_in[0], edge_in[1]], axis=0)
    border_proj = dot(border, w_send[...]).astype(BF16)
    table[0:BORDER, :] = border_proj[:BORDER]
    table[BORDER + nodes : span, :] = border_proj[BORDER:]

    def add_messages(pre, slab_rows):
        message = normalize(dot(silu(pre).astype(BF16), w_message[...])).astype(BF16)
        total[...] += dot(one_hot_rows(slab_rows.astype(jnp.int32), nodes), message)

    loops = edges // CHUNK
    steps = [functools.partial(step_z, step) for step in range(1, line)] + [step_y]
    turns = [[] for _ in range(loops)]
    for number, step in enumerate(steps):
        turns[number * loops // len(steps)].append(step)

    def fine(i, carry):
        for number, group_of in enumerate(turns):
            if group_of:

                @pl.when(i == number)
                def _():
                    for step in group_of:
                        step()

        at = pl.ds(pl.multiple_of(i * CHUNK, CHUNK), CHUNK)
        slab = slab_fine[:, at]
        turned = turn(slab)
        place = turned[:, 0:2].astype(jnp.int32)
        pick = jnp.concatenate(
            [one_hot(place[:, 0:1], span), one_hot(place[:, 1:2], nodes), turned.astype(BF16)],
            axis=1,
        )
        add_messages(dot(pick, table[...]), slab[1:2, :])
        return carry

    lax.fori_loop(0, loops, fine, 0)

    step_end()
    coarse_table[...] = dot(
        coarse[...].reshape(regions * COARSE, width), w_send[...]
    ).astype(BF16)
    reach = owners * COARSE
    for number in range(slots // group):
        slab = slab_long[:, number * group : (number + 1) * group]
        turned = turn(slab)
        place = turned[:, 0:2].astype(jnp.int32)
        near = jnp.concatenate([one_hot(place[:, 1:2], nodes), turned.astype(BF16)], axis=1)
        pre = dot(
            one_hot(place[:, 0:1], reach), coarse_table[number * reach : (number + 1) * reach, :]
        ) + dot(near, table[span:, :])
        add_messages(pre, slab[1:2, :])

    load(3).wait()
    load(4).wait()

    def refresh(aggregate, own_part, latent):
        hidden = silu(own_part + dot(aggregate.astype(BF16), w_node_agg[...])).astype(BF16)
        return (latent.astype(F32) + dot(hidden, w_node_out[...])).astype(BF16)

    def both(ref):
        return jnp.concatenate([ref[:BORDER, :], ref[nodes - BORDER :, :]], axis=0)

    ends = refresh(both(total), both(self_part), both(node))
    ends_out[0] = ends[:BORDER]
    ends_out[1] = ends[BORDER:]
    exchange(ends_out.at[0], ends_out.at[1], 1, ends_in)
    inner = slice(BORDER, nodes - BORDER)
    out_mesh[inner, :] = refresh(total[inner, :], self_part[inner, :], node[inner, :])
    out_mesh[:BORDER, :] = ends[:BORDER]
    out_mesh[nodes - BORDER :, :] = ends[BORDER:]
    for number in (5, 0, 6, 9):
        load(number).wait()
    dec_table[BORDER : BORDER + nodes, :] = dot(out_mesh[...], w_dec_send[...]).astype(BF16)
    grid_part[...] = dot(grid[...], w_dec_grid[...])
    grid_own[...] = dot(grid[...], w_grid_self[...])
    for number in (7, 8, 10):
        load(number).wait()
    settle(ends_out.at[0], ends_out.at[1], 1, ends_in)
    border = jnp.concatenate([ends_in[0], ends_in[1]], axis=0)
    border_proj = dot(border, w_dec_send[...]).astype(BF16)
    dec_table[0:BORDER, :] = border_proj[:BORDER]
    dec_table[BORDER + nodes : span, :] = border_proj[BORDER:]

    part = points // 2

    for number in range(2):
        at = pl.ds(number * part, part)
        picks = []
        for k in range(3):
            turned = turn(slab_dec[k, :, at])
            place = turned[:, 0:1].astype(jnp.int32)
            picks.append(jnp.concatenate([one_hot(place, span), turned.astype(BF16)], axis=1))
        pick = jnp.concatenate(picks, axis=0)
        grid_three = jnp.concatenate([grid_part[at, :]] * 3, axis=0)
        pre = dot(pick, dec_table[...]) + grid_three
        message = normalize(dot(silu(pre).astype(BF16), w_dec_final[...]))
        gathered = message[:part] + message[part : 2 * part] + message[2 * part :]
        hidden = silu(dot(gathered.astype(BF16), w_grid_agg[...]) + grid_own[at, :])
        fields = lax.dot_general(
            w_final[...],
            hidden.astype(BF16),
            (((1,), (1,)), ((), ())),
            preferred_element_type=F32,
        )
        out_fields[:, at] = fields.astype(BF16)


def body(
    node_latent,
    grid_latent,
    fine_edge_sender,
    short_recv,
    short_geo,
    long_send,
    long_recv,
    long_geo,
    dec_send,
    dec_geo,
    w_send,
    w_recv,
    w_edge_geo,
    w_message,
    w_node_self,
    w_node_agg,
    w_node_out,
    w_dec_send,
    w_dec_grid,
    w_dec_geo,
    decoding_link_final_matrix,
    w_grid_agg,
    w_grid_self,
    final_projection_matrix,
):
    regions = lax.axis_size("region")
    nodes, width = node_latent.shape
    points = grid_latent.shape[0]
    edges, slots = fine_edge_sender.shape[0], long_send.shape[0]
    line = regions // 4
    fields = final_projection_matrix.shape[0]
    span = nodes + 2 * BORDER
    square = pltpu.VMEM((width, width), BF16)
    vmem = pl.BlockSpec(memory_space=pltpu.VMEM)
    anywhere = pl.BlockSpec(memory_space=pl.ANY)
    dma = pltpu.SemaphoreType.DMA

    def lanes(array):
        return array.reshape(-1, LANES)

    return pl.pallas_call(
        functools.partial(kernel, regions),
        out_shape=(
            jax.ShapeDtypeStruct((nodes, width), BF16),
            jax.ShapeDtypeStruct((fields, points), BF16),
        ),
        in_specs=[vmem, anywhere] + [vmem] * 12 + [anywhere] * 10,
        out_specs=(vmem, vmem),
        scratch_shapes=[pltpu.VMEM((points, width), BF16)]
        + [square] * 9
        + [
            pltpu.VMEM((fields, width), BF16),
            dma((11,)),
            pltpu.VMEM((2, BORDER, width), BF16),
            pltpu.VMEM((2, BORDER, width), BF16),
            pltpu.VMEM((2, BORDER, width), BF16),
            dma((2, 2)),
            dma((2, 2)),
            pltpu.VMEM((regions, COARSE, width), BF16),
            dma((2, line)),
            dma((2, line)),
            dma((line,)),
            dma((line,)),
            dma((2, line)),
            dma((2, line)),
            pltpu.VMEM((span + nodes + TAIL, width), BF16),
            pltpu.VMEM((regions * COARSE, width), BF16),
            pltpu.VMEM((span + TAIL, width), BF16),
            pltpu.VMEM((16, edges), F32),
            pltpu.VMEM((16, slots), F32),
            pltpu.VMEM((3, 16, points), F32),
            pltpu.VMEM((nodes, width), F32),
            pltpu.VMEM((nodes, width), F32),
            pltpu.VMEM((points, width), F32),
            pltpu.VMEM((points, width), F32),
        ],
        compiler_params=pltpu.CompilerParams(
            collective_id=0, has_side_effects=True, vmem_limit_bytes=56 * 1024 * 1024
        ),
        name="graph_round",
    )(
        node_latent,
        grid_latent,
        lanes(fine_edge_sender),
        lanes(short_recv),
        short_geo,
        lanes(long_send),
        lanes(long_recv),
        long_geo,
        dec_send,
        dec_geo,
        w_send,
        w_recv,
        w_edge_geo,
        w_dec_geo,
        w_message,
        w_node_self,
        w_node_agg,
        w_node_out,
        w_dec_send,
        w_dec_grid,
        decoding_link_final_matrix,
        w_grid_agg,
        w_grid_self,
        final_projection_matrix,
    )


def solution(mesh):
    split = ("ens", "region")
    in_specs = (
        P(split, None),
        P(split, None),
        P(split),
        P(split),
        P(None, split),
        P(split),
        P(split),
        P(None, split),
        P(None, split),
        P(None, None, split),
    ) + (P(),) * 14
    out_specs = (P(split, None), P(None, split))
    return jax.shard_map(body, mesh=mesh, in_specs=in_specs, out_specs=out_specs, check_vma=False)
```

```python
import functools

import jax
import jax.numpy as jnp
from jax import lax
from jax.experimental import pallas as pl
from jax.experimental.pallas import tpu as pltpu
from jax.sharding import PartitionSpec as P

BORDER = 64
COARSE = 64
TAIL = 128
LANES = 128
CHUNK = 512
F32 = jnp.float32
BF16 = jnp.bfloat16
MESH = pl.DeviceIdType.MESH


def dot(left, right):
    return jnp.dot(left, right, preferred_element_type=F32)


def silu(value):
    half = 0.5 * value
    return half + half * jnp.tanh(half)


def normalize(values):
    width = 1.0 / values.shape[-1]
    centred = values - jnp.sum(values, axis=-1, keepdims=True) * width
    spread = jnp.sum(centred * centred, axis=-1, keepdims=True) * width
    return centred * lax.rsqrt(spread + 1e-5)


def one_hot(place, count):
    lanes = lax.broadcasted_iota(jnp.int32, (place.shape[0], count), 1)
    return jnp.where(lanes == place, 1.0, 0.0).astype(BF16)


def one_hot_rows(place, count):
    rows = lax.broadcasted_iota(jnp.int32, (count, place.shape[1]), 0)
    return jnp.where(rows == place, 1.0, 0.0).astype(BF16)


def turn(slab):
    parts = []
    for start in range(0, slab.shape[1], LANES):
        piece = slab[:, start : start + LANES]
        full = jnp.concatenate([piece, jnp.zeros((LANES - 16, LANES), F32)], axis=0)
        parts.append(full.T)
    return jnp.concatenate(parts, axis=0)


def put_geometry(slab, geo):
    high = geo.astype(BF16).astype(F32)
    slab[4:8, :] = high
    slab[8:12, :] = geo - high
    slab[12:16, :] = high


def put_tail(table, start, w_geo):
    high = w_geo.astype(BF16).astype(F32)
    width = w_geo.shape[1]
    rows = jnp.concatenate(
        [jnp.zeros((4, width), F32), high, high, w_geo - high, jnp.zeros((TAIL - 16, width), F32)],
        axis=0,
    )
    table[start : start + TAIL, :] = rows.astype(BF16)


def kernel(
    regions,
    node,
    grid_hbm,
    fine_send,
    fine_recv,
    fine_geo,
    long_send,
    long_recv,
    long_geo,
    dec_send,
    dec_geo,
    w_send,
    w_recv,
    w_edge_geo,
    w_dec_geo,
    w_message_hbm,
    w_node_self_hbm,
    w_node_agg_hbm,
    w_node_out_hbm,
    w_dec_send_hbm,
    w_dec_grid_hbm,
    w_dec_final_hbm,
    w_grid_agg_hbm,
    w_grid_self_hbm,
    w_final_hbm,
    out_mesh,
    out_fields,
    grid,
    w_message,
    w_node_self,
    w_node_agg,
    w_node_out,
    w_dec_send,
    w_dec_grid,
    w_dec_final,
    w_grid_agg,
    w_grid_self,
    w_final,
    load_sem,
    edge_in,
    ends_out,
    ends_in,
    border_send,
    border_recv,
    coarse,
    z_send,
    z_recv,
    y_send,
    y_recv,
    c_send,
    c_recv,
    table,
    coarse_table,
    dec_table,
    slab_fine,
    slab_long,
    slab_dec,
    total,
    self_part,
    grid_part,
    grid_own,
    hidden,
    picks,
):
    nodes, width = node.shape
    edges = slab_fine.shape[1]
    slots = slab_long.shape[1]
    points = slab_dec.shape[2]
    span = nodes + 2 * BORDER
    ens = lax.axis_index("ens")
    me = lax.axis_index("region")
    line = regions // 4
    spot = me // 4
    lane = me % 4
    twin = me + 1 - 2 * (me % 2)
    side = lane % 4
    across = me + 2 - 4 * (side // 2)

    loads = [
        (grid_hbm, grid),
        (w_message_hbm, w_message),
        (w_node_self_hbm, w_node_self),
        (w_node_agg_hbm, w_node_agg),
        (w_node_out_hbm, w_node_out),
        (w_dec_send_hbm, w_dec_send),
        (w_dec_grid_hbm, w_dec_grid),
        (w_dec_final_hbm, w_dec_final),
        (w_grid_agg_hbm, w_grid_agg),
        (w_grid_self_hbm, w_grid_self),
        (w_final_hbm, w_final),
    ]

    def load(number):
        return pltpu.make_async_copy(*loads[number], load_sem.at[number])

    for number in (1, 2, 0, 3, 4, 5, 6, 7, 8, 9, 10):
        load(number).start()

    has_left, has_right = me > 0, me < regions - 1
    has_back, has_next = spot > 0, spot < line - 1

    barrier = pltpu.get_barrier_semaphore()

    def greet(other):
        pl.semaphore_signal(barrier, inc=1, device_id=(ens, other), device_id_type=MESH)

    greet(across)
    for present, other in (
        (has_left, me - 1),
        (has_right, me + 1),
        (has_back, me - 4),
        (has_next, me + 4),
    ):
        pl.when(present)(functools.partial(greet, other))
    coarse[me] = node[:COARSE, :]
    count = 1
    for present in (has_left, has_right, has_back, has_next):
        count = count + present.astype(jnp.int32)
    pl.semaphore_wait(barrier, count)

    def remote(src, dst, send, recv, other):
        return pltpu.make_async_remote_copy(
            src_ref=src,
            dst_ref=dst,
            send_sem=send,
            recv_sem=recv,
            device_id=(ens, other),
            device_id_type=MESH,
        )

    def border_up(src, phase, into):
        return remote(
            src, into.at[0], border_send.at[phase, 0], border_recv.at[phase, 0], me + 1
        )

    def border_down(src, phase, into):
        return remote(
            src, into.at[1], border_send.at[phase, 1], border_recv.at[phase, 1], me - 1
        )

    def exchange(first, last, phase, into):
        pl.when(has_right)(lambda: border_up(last, phase, into).start())
        pl.when(has_left)(lambda: border_down(first, phase, into).start())

        @pl.when(jnp.logical_not(has_left))
        def _():
            into[0] = jnp.zeros((BORDER, width), BF16)

        @pl.when(jnp.logical_not(has_right))
        def _():
            into[1] = jnp.zeros((BORDER, width), BF16)

    def settle(first, last, phase, into):
        @pl.when(has_right)
        def _():
            border_up(last, phase, into).wait_send()
            border_down(first, phase, into).wait_recv()

        @pl.when(has_left)
        def _():
            border_down(first, phase, into).wait_send()
            border_up(last, phase, into).wait_recv()

    node_first, node_last = node.at[pl.ds(0, BORDER)], node.at[pl.ds(nodes - BORDER, BORDER)]
    exchange(node_first, node_last, 0, edge_in)

    def z_copy(way, step, place):
        block = coarse.at[place * 4 + lane]
        other = me + 4 - 8 * way
        return remote(block, block, z_send.at[way, step], z_recv.at[way, step], other)

    def y_copy(place):
        block = coarse.at[place * 4 + lane]
        return remote(block, block, y_send.at[place], y_recv.at[place], across)

    def c_copy(half, place):
        block = coarse.at[place * 4 + (lane + 2 * half) % 4]
        return remote(block, block, c_send.at[half, place], c_recv.at[half, place], twin)

    def spread(place):
        y_copy(place).start()
        c_copy(0, place).start()

    def step_z(step):
        for way in range(2):
            place = spot - step if way == 0 else spot + step
            held = (place >= 0) & (place < line)

            @pl.when(held)
            def _():
                if step > 0:
                    z_copy(way, step - 1, place).wait_recv()
                if step < line - 1:
                    onward = has_next if way == 0 else has_back
                    pl.when(onward)(lambda: z_copy(way, step, place).start())
                if step > 0:
                    spread(place)

    def step_y():
        for place in range(line):
            y_copy(place).wait_recv()
            c_copy(1, place).start()

    def step_end():
        for place in range(line):
            for half in range(2):
                c_copy(half, place).wait()
            y_copy(place).wait_send()
        for step in range(line - 1):
            for way in range(2):
                place = spot - step if way == 0 else spot + step
                onward = has_next if way == 0 else has_back
                held = (place >= 0) & (place < line) & onward
                pl.when(held)(lambda: z_copy(way, step, place).wait_send())

    step_z(0)

    own = node[...]
    table[BORDER : BORDER + nodes, :] = dot(own, w_send[...]).astype(BF16)
    table[span : span + nodes, :] = dot(own, w_recv[...]).astype(BF16)
    put_tail(table, span + nodes, w_edge_geo[...])
    put_tail(dec_table, span, w_dec_geo[...])
    offset = me * nodes - BORDER
    for slab, geo in ((slab_fine, fine_geo[...]), (slab_long, long_geo[...])):
        put_geometry(slab, geo)
        slab[2:4, :] = jnp.zeros((2, geo.shape[1]), F32)
    for row in range(edges // LANES):
        at = pl.ds(row * LANES, LANES)
        slab_fine[0:1, at] = (fine_send[row : row + 1, :] - offset).astype(F32)
        slab_fine[1:2, at] = fine_recv[row : row + 1, :].astype(F32)
    per_owner = slots // regions
    group = max(per_owner, slots // 2)
    owners = group // per_owner
    for row in range(slots // LANES):
        at = pl.ds(row * LANES, LANES)
        slot = lax.broadcasted_iota(jnp.int32, (1, LANES), 1) + row * LANES
        owner = slot // per_owner
        sender = long_send[row : row + 1, :]
        base = (row * LANES // group) * owners
        within = sender - owner * nodes + (owner - base) * COARSE
        full = sender >= 0
        slab_long[0:1, at] = jnp.where(full, within, -1).astype(F32)
        slab_long[1:2, at] = jnp.where(full, long_recv[row : row + 1, :], -1).astype(F32)
    for k in range(3):
        slab_dec[k, 0:1, :] = (dec_send[k : k + 1, :] - offset).astype(F32)
        slab_dec[k, 1:4, :] = jnp.zeros((3, points), F32)
        for i in range(4):
            geo = dec_geo[k, i : i + 1, :]
            high = geo.astype(BF16).astype(F32)
            slab_dec[k, 4 + i : 5 + i, :] = high
            slab_dec[k, 8 + i : 9 + i, :] = geo - high
            slab_dec[k, 12 + i : 13 + i, :] = high
    total[...] = jnp.zeros(total.shape, F32)
    load(2).wait()
    self_part[...] = dot(own, w_node_self[...])
    load(1).wait()

    load(0).wait()
    load(6).wait()
    grid_part[...] = dot(grid[...], w_dec_grid[...])

    def pick_fine(slab):
        turned = turn(slab)
        place = turned[:, 0:2].astype(jnp.int32)
        return jnp.concatenate(
            [one_hot(place[:, 0:1], span), one_hot(place[:, 1:2], nodes), turned.astype(BF16)],
            axis=1,
        )

    settle(node_first, node_last, 0, edge_in)
    spread(spot)
    border = jnp.concatenate([edge_in[0], edge_in[1]], axis=0)
    border_proj = dot(border, w_send[...]).astype(BF16)
    table[0:BORDER, :] = border_proj[:BORDER]
    table[BORDER + nodes : span, :] = border_proj[BORDER:]

    def message_of(held):
        return normalize(dot(held, w_message[...])).astype(BF16)

    def add(place, message):
        total[...] += dot(one_hot_rows(place.astype(jnp.int32), nodes), message)

    loops = edges // CHUNK
    steps = [functools.partial(step_z, step) for step in range(1, line)]
    turns = [[] for _ in range(loops)]
    for number, step in enumerate(steps):
        turns[1 + number * (loops - 1) // len(steps)].append(step)

    hidden[...] = silu(dot(pick_fine(slab_fine[:, :CHUNK]), table[...])).astype(BF16)

    def fine(i, carry):
        for number, group_of in enumerate(turns):
            if group_of:

                @pl.when(i == number)
                def _():
                    for step in group_of:
                        step()

        at = pl.ds(pl.multiple_of(i * CHUNK, CHUNK), CHUNK)
        before = pl.ds(pl.multiple_of((i - 1) * CHUNK, CHUNK), CHUNK)
        held = dot(hidden[...], w_message[...])
        pre = dot(pick_fine(slab_fine[:, at]), table[...])
        add(slab_fine[1:2, before], normalize(held).astype(BF16))
        hidden[...] = silu(pre).astype(BF16)
        return carry

    lax.fori_loop(1, loops, fine, 0)
    step_y()
    add(slab_fine[1:2, edges - CHUNK :], message_of(hidden[...]))
    load(9).wait()
    grid_own[...] = dot(grid[...], w_grid_self[...])
    step_end()
    coarse_table[...] = dot(
        coarse[...].reshape(regions * COARSE, width), w_send[...]
    ).astype(BF16)
    reach = owners * COARSE
    for number in range(slots // group):
        slab = slab_long[:, number * group : (number + 1) * group]
        turned = turn(slab)
        place = turned[:, 0:2].astype(jnp.int32)
        near = jnp.concatenate([one_hot(place[:, 1:2], nodes), turned.astype(BF16)], axis=1)
        pre = dot(
            one_hot(place[:, 0:1], reach), coarse_table[number * reach : (number + 1) * reach, :]
        ) + dot(near, table[span:, :])
        add(slab[1:2, :], message_of(silu(pre).astype(BF16)))

    load(3).wait()
    load(4).wait()

    def refresh(aggregate, own_part, latent):
        hidden = silu(own_part + dot(aggregate.astype(BF16), w_node_agg[...])).astype(BF16)
        return (latent.astype(F32) + dot(hidden, w_node_out[...])).astype(BF16)

    def both(ref):
        return jnp.concatenate([ref[:BORDER, :], ref[nodes - BORDER :, :]], axis=0)

    ends = refresh(both(total), both(self_part), both(node))
    ends_out[0] = ends[:BORDER]
    ends_out[1] = ends[BORDER:]
    exchange(ends_out.at[0], ends_out.at[1], 1, ends_in)
    inner = slice(BORDER, nodes - BORDER)
    out_mesh[inner, :] = refresh(total[inner, :], self_part[inner, :], node[inner, :])
    out_mesh[:BORDER, :] = ends[:BORDER]
    out_mesh[nodes - BORDER :, :] = ends[BORDER:]
    load(5).wait()
    dec_table[BORDER : BORDER + nodes, :] = dot(out_mesh[...], w_dec_send[...]).astype(BF16)
    part = points // 2
    for number in range(2):
        for k in range(3):
            turned = turn(slab_dec[k, :, number * part : (number + 1) * part])
            place = turned[:, 0:1].astype(jnp.int32)
            rows = pl.ds(k * part, part)
            picks[number, rows, :span] = one_hot(place, span)
            picks[number, rows, span:] = turned.astype(BF16)
    for number in (7, 8, 10):
        load(number).wait()
    settle(ends_out.at[0], ends_out.at[1], 1, ends_in)
    border = jnp.concatenate([ends_in[0], ends_in[1]], axis=0)
    border_proj = dot(border, w_dec_send[...]).astype(BF16)
    dec_table[0:BORDER, :] = border_proj[:BORDER]
    dec_table[BORDER + nodes : span, :] = border_proj[BORDER:]

    for number in range(2):
        at = pl.ds(number * part, part)
        grid_three = jnp.concatenate([grid_part[at, :]] * 3, axis=0)
        pre = dot(picks[number], dec_table[...]) + grid_three
        message = normalize(dot(silu(pre).astype(BF16), w_dec_final[...]))
        gathered = message[:part] + message[part : 2 * part] + message[2 * part :]
        state = silu(dot(gathered.astype(BF16), w_grid_agg[...]) + grid_own[at, :])
        fields = lax.dot_general(
            w_final[...],
            state.astype(BF16),
            (((1,), (1,)), ((), ())),
            preferred_element_type=F32,
        )
        out_fields[:, at] = fields.astype(BF16)


def hand_over(mesh_in, fields_in, mesh_out, fields_out, sems):
    quarter = mesh_in.shape[0] // 4
    copies = [
        pltpu.make_async_copy(
            mesh_in.at[pl.ds(i * quarter, quarter)], mesh_out.at[pl.ds(i * quarter, quarter)], sems.at[i]
        )
        for i in range(4)
    ] + [pltpu.make_async_copy(fields_in, fields_out, sems.at[4])]
    for copy in copies:
        copy.start()
    for copy in copies:
        copy.wait()


def body(
    node_latent,
    grid_latent,
    fine_edge_sender,
    short_recv,
    short_geo,
    long_send,
    long_recv,
    long_geo,
    dec_send,
    dec_geo,
    w_send,
    w_recv,
    w_edge_geo,
    w_message,
    w_node_self,
    w_node_agg,
    w_node_out,
    w_dec_send,
    w_dec_grid,
    w_dec_geo,
    decoding_link_final_matrix,
    w_grid_agg,
    w_grid_self,
    final_projection_matrix,
):
    regions = lax.axis_size("region")
    nodes, width = node_latent.shape
    points = grid_latent.shape[0]
    edges, slots = fine_edge_sender.shape[0], long_send.shape[0]
    line = regions // 4
    fields = final_projection_matrix.shape[0]
    span = nodes + 2 * BORDER
    square = pltpu.VMEM((width, width), BF16)
    vmem = pl.BlockSpec(memory_space=pltpu.VMEM)
    anywhere = pl.BlockSpec(memory_space=pl.ANY)
    dma = pltpu.SemaphoreType.DMA

    def lanes(array):
        return array.reshape(-1, LANES)

    results = pl.pallas_call(
        functools.partial(kernel, regions),
        out_shape=(
            jax.ShapeDtypeStruct((nodes, width), BF16),
            jax.ShapeDtypeStruct((fields, points), BF16),
        ),
        in_specs=[vmem, anywhere] + [vmem] * 12 + [anywhere] * 10,
        out_specs=(vmem, vmem),
        scratch_shapes=[pltpu.VMEM((points, width), BF16)]
        + [square] * 9
        + [
            pltpu.VMEM((fields, width), BF16),
            dma((11,)),
            pltpu.VMEM((2, BORDER, width), BF16),
            pltpu.VMEM((2, BORDER, width), BF16),
            pltpu.VMEM((2, BORDER, width), BF16),
            dma((2, 2)),
            dma((2, 2)),
            pltpu.VMEM((regions, COARSE, width), BF16),
            dma((2, line)),
            dma((2, line)),
            dma((line,)),
            dma((line,)),
            dma((2, line)),
            dma((2, line)),
            pltpu.VMEM((span + nodes + TAIL, width), BF16),
            pltpu.VMEM((regions * COARSE, width), BF16),
            pltpu.VMEM((span + TAIL, width), BF16),
            pltpu.VMEM((16, edges), F32),
            pltpu.VMEM((16, slots), F32),
            pltpu.VMEM((3, 16, points), F32),
            pltpu.VMEM((nodes, width), F32),
            pltpu.VMEM((nodes, width), F32),
            pltpu.VMEM((points, width), F32),
            pltpu.VMEM((points, width), F32),
            pltpu.VMEM((CHUNK, width), BF16),
            pltpu.VMEM((2, 3 * (points // 2), span + TAIL), BF16),
        ],
        compiler_params=pltpu.CompilerParams(
            collective_id=0, has_side_effects=True, vmem_limit_bytes=56 * 1024 * 1024
        ),
        name="graph_round",
    )(
        node_latent,
        grid_latent,
        lanes(fine_edge_sender),
        lanes(short_recv),
        short_geo,
        lanes(long_send),
        lanes(long_recv),
        long_geo,
        dec_send,
        jnp.transpose(dec_geo, (1, 0, 2)),
        w_send,
        w_recv,
        w_edge_geo,
        w_dec_geo,
        w_message,
        w_node_self,
        w_node_agg,
        w_node_out,
        w_dec_send,
        w_dec_grid,
        decoding_link_final_matrix,
        w_grid_agg,
        w_grid_self,
        final_projection_matrix,
    )
    return pl.pallas_call(
        hand_over,
        out_shape=tuple(jax.ShapeDtypeStruct(array.shape, array.dtype) for array in results),
        in_specs=[anywhere] * 2,
        out_specs=(anywhere,) * 2,
        scratch_shapes=[dma((5,))],
        compiler_params=pltpu.CompilerParams(vmem_limit_bytes=56 * 1024 * 1024),
        name="hand_over",
    )(*results)


def solution(mesh):
    split = ("ens", "region")
    in_specs = (
        P(split, None),
        P(split, None),
        P(split),
        P(split),
        P(None, split),
        P(split),
        P(split),
        P(None, split),
        P(None, split),
        P(None, None, split),
    ) + (P(),) * 14
    out_specs = (P(split, None), P(None, split))
    return jax.shard_map(body, mesh=mesh, in_specs=in_specs, out_specs=out_specs, check_vma=False)
```

```python
import functools

import jax
import jax.numpy as jnp
from jax import lax
from jax.experimental import pallas as pl
from jax.experimental.pallas import tpu as pltpu
from jax.sharding import PartitionSpec as P

BORDER = 64
COARSE = 64
TAIL = 128
LANES = 128
CHUNK = 512
F32 = jnp.float32
BF16 = jnp.bfloat16
MESH = pl.DeviceIdType.MESH


def dot(left, right):
    return jnp.dot(left, right, preferred_element_type=F32)


def silu(value):
    half = 0.5 * value
    return half + half * jnp.tanh(half)


def normalize(values):
    width = 1.0 / values.shape[-1]
    centred = values - jnp.sum(values, axis=-1, keepdims=True) * width
    spread = jnp.sum(centred * centred, axis=-1, keepdims=True) * width
    return centred * lax.rsqrt(spread + 1e-5)


def one_hot(place, count):
    lanes = lax.broadcasted_iota(jnp.int32, (place.shape[0], count), 1)
    return jnp.where(lanes == place, 1.0, 0.0).astype(BF16)


def one_hot_rows(place, count):
    rows = lax.broadcasted_iota(jnp.int32, (count, place.shape[1]), 0)
    return jnp.where(rows == place, 1.0, 0.0).astype(BF16)


def turn(slab):
    blocks = slab.shape[1] // LANES
    pieces = [slab[:, i * LANES : (i + 1) * LANES] for i in range(blocks)]
    if blocks < LANES // 16:
        pieces.append(jnp.zeros((LANES - 16 * blocks, LANES), F32))
    turned = jnp.concatenate(pieces, axis=0).T
    lanes = lax.broadcasted_iota(jnp.int32, (LANES, LANES), 1)
    parts = [
        jnp.where((lanes >= 16 * i) & (lanes < 16 * i + 16), turned, 0.0) for i in range(blocks)
    ]
    places = [
        jnp.concatenate(
            [turned[:, 16 * i + j : 16 * i + j + 1] for i in range(blocks)], axis=0
        ).astype(jnp.int32)
        for j in range(2)
    ]
    return jnp.concatenate(parts, axis=0).astype(BF16), places[0], places[1]


def put_geometry(slab, geo):
    high = geo.astype(BF16).astype(F32)
    slab[4:8, :] = high
    slab[8:12, :] = geo - high
    slab[12:16, :] = high


def put_tail(table, start, w_geo):
    high = w_geo.astype(BF16).astype(F32)
    width = w_geo.shape[1]
    rows = jnp.concatenate(
        [jnp.zeros((4, width), F32), high, high, w_geo - high] * (TAIL // 16), axis=0
    )
    table[start : start + TAIL, :] = rows.astype(BF16)


def kernel(
    regions,
    node,
    grid_hbm,
    fine_send,
    fine_recv,
    fine_geo,
    long_send,
    long_recv,
    long_geo,
    dec_send,
    dec_geo,
    w_send,
    w_recv,
    w_edge_geo,
    w_dec_geo,
    w_message_hbm,
    w_node_self_hbm,
    w_node_agg_hbm,
    w_node_out_hbm,
    w_dec_send_hbm,
    w_dec_grid_hbm,
    w_dec_final_hbm,
    w_grid_agg_hbm,
    w_grid_self_hbm,
    w_final_hbm,
    out_mesh,
    out_fields,
    grid,
    w_message,
    w_node_self,
    w_node_agg,
    w_node_out,
    w_dec_send,
    w_dec_grid,
    w_dec_final,
    w_grid_agg,
    w_grid_self,
    w_final,
    load_sem,
    edge_in,
    ends_out,
    ends_in,
    border_send,
    border_recv,
    coarse,
    z_send,
    z_recv,
    y_send,
    y_recv,
    c_send,
    c_recv,
    table,
    coarse_table,
    dec_table,
    slab_fine,
    slab_long,
    slab_dec,
    total,
    self_part,
    grid_part,
    grid_own,
    hidden,
    picks,
):
    nodes, width = node.shape
    edges = slab_fine.shape[1]
    slots = slab_long.shape[1]
    points = slab_dec.shape[2]
    span = nodes + 2 * BORDER
    ens = lax.axis_index("ens")
    me = lax.axis_index("region")
    line = regions // 4
    spot = me // 4
    lane = me % 4
    twin = me + 1 - 2 * (me % 2)
    side = lane % 4
    across = me + 2 - 4 * (side // 2)

    loads = [
        (grid_hbm, grid),
        (w_message_hbm, w_message),
        (w_node_self_hbm, w_node_self),
        (w_node_agg_hbm, w_node_agg),
        (w_node_out_hbm, w_node_out),
        (w_dec_send_hbm, w_dec_send),
        (w_dec_grid_hbm, w_dec_grid),
        (w_dec_final_hbm, w_dec_final),
        (w_grid_agg_hbm, w_grid_agg),
        (w_grid_self_hbm, w_grid_self),
        (w_final_hbm, w_final),
    ]

    def load(number):
        return pltpu.make_async_copy(*loads[number], load_sem.at[number])

    for number in (1, 2, 0, 3, 4, 5, 6, 7, 8, 9, 10):
        load(number).start()

    has_left, has_right = me > 0, me < regions - 1
    has_back, has_next = spot > 0, spot < line - 1

    barrier = pltpu.get_barrier_semaphore()

    def greet(other):
        pl.semaphore_signal(barrier, inc=1, device_id=(ens, other), device_id_type=MESH)

    greet(across)
    for present, other in (
        (has_left, me - 1),
        (has_right, me + 1),
        (has_back, me - 4),
        (has_next, me + 4),
    ):
        pl.when(present)(functools.partial(greet, other))
    coarse[me] = node[:COARSE, :]
    count = 1
    for present in (has_left, has_right, has_back, has_next):
        count = count + present.astype(jnp.int32)
    pl.semaphore_wait(barrier, count)

    def remote(src, dst, send, recv, other):
        return pltpu.make_async_remote_copy(
            src_ref=src,
            dst_ref=dst,
            send_sem=send,
            recv_sem=recv,
            device_id=(ens, other),
            device_id_type=MESH,
        )

    def border_up(src, phase, into):
        return remote(
            src, into.at[0], border_send.at[phase, 0], border_recv.at[phase, 0], me + 1
        )

    def border_down(src, phase, into):
        return remote(
            src, into.at[1], border_send.at[phase, 1], border_recv.at[phase, 1], me - 1
        )

    def exchange(first, last, phase, into):
        pl.when(has_right)(lambda: border_up(last, phase, into).start())
        pl.when(has_left)(lambda: border_down(first, phase, into).start())

        @pl.when(jnp.logical_not(has_left))
        def _():
            into[0] = jnp.zeros((BORDER, width), BF16)

        @pl.when(jnp.logical_not(has_right))
        def _():
            into[1] = jnp.zeros((BORDER, width), BF16)

    def settle(first, last, phase, into):
        @pl.when(has_right)
        def _():
            border_up(last, phase, into).wait_send()
            border_down(first, phase, into).wait_recv()

        @pl.when(has_left)
        def _():
            border_down(first, phase, into).wait_send()
            border_up(last, phase, into).wait_recv()

    node_first, node_last = node.at[pl.ds(0, BORDER)], node.at[pl.ds(nodes - BORDER, BORDER)]
    exchange(node_first, node_last, 0, edge_in)

    def z_copy(way, step, place):
        block = coarse.at[place * 4 + lane]
        other = me + 4 - 8 * way
        return remote(block, block, z_send.at[way, step], z_recv.at[way, step], other)

    def y_copy(place):
        block = coarse.at[place * 4 + lane]
        return remote(block, block, y_send.at[place], y_recv.at[place], across)

    def c_copy(half, place):
        block = coarse.at[place * 4 + (lane + 2 * half) % 4]
        return remote(block, block, c_send.at[half, place], c_recv.at[half, place], twin)

    def spread(place):
        y_copy(place).start()
        c_copy(0, place).start()

    def step_z(step):
        for way in range(2):
            place = spot - step if way == 0 else spot + step
            held = (place >= 0) & (place < line)

            @pl.when(held)
            def _():
                if step > 0:
                    z_copy(way, step - 1, place).wait_recv()
                if step < line - 1:
                    onward = has_next if way == 0 else has_back
                    pl.when(onward)(lambda: z_copy(way, step, place).start())
                if step > 0:
                    spread(place)

    def step_y():
        for place in range(line):
            y_copy(place).wait_recv()
            c_copy(1, place).start()

    def step_end():
        for place in range(line):
            for half in range(2):
                c_copy(half, place).wait()
            y_copy(place).wait_send()
        for step in range(line - 1):
            for way in range(2):
                place = spot - step if way == 0 else spot + step
                onward = has_next if way == 0 else has_back
                held = (place >= 0) & (place < line) & onward
                pl.when(held)(lambda: z_copy(way, step, place).wait_send())

    step_z(0)

    own = node[...]
    table[BORDER : BORDER + nodes, :] = dot(own, w_send[...]).astype(BF16)
    table[span : span + nodes, :] = dot(own, w_recv[...]).astype(BF16)
    put_tail(table, span + nodes, w_edge_geo[...])
    put_tail(dec_table, span, w_dec_geo[...])
    offset = me * nodes - BORDER
    for slab, geo in ((slab_fine, fine_geo[...]), (slab_long, long_geo[...])):
        put_geometry(slab, geo)
        slab[2:4, :] = jnp.zeros((2, geo.shape[1]), F32)
    for row in range(edges // LANES):
        at = pl.ds(row * LANES, LANES)
        slab_fine[0:1, at] = (fine_send[row : row + 1, :] - offset).astype(F32)
        slab_fine[1:2, at] = fine_recv[row : row + 1, :].astype(F32)
    per_owner = slots // regions
    group = max(per_owner, slots // 2)
    owners = group // per_owner
    for row in range(slots // LANES):
        at = pl.ds(row * LANES, LANES)
        slot = lax.broadcasted_iota(jnp.int32, (1, LANES), 1) + row * LANES
        owner = slot // per_owner
        sender = long_send[row : row + 1, :]
        base = (row * LANES // group) * owners
        within = sender - owner * nodes + (owner - base) * COARSE
        full = sender >= 0
        slab_long[0:1, at] = jnp.where(full, within, -1).astype(F32)
        slab_long[1:2, at] = jnp.where(full, long_recv[row : row + 1, :], -1).astype(F32)
    for k in range(3):
        slab_dec[k, 0:1, :] = (dec_send[k : k + 1, :] - offset).astype(F32)
        slab_dec[k, 1:4, :] = jnp.zeros((3, points), F32)
        for i in range(4):
            geo = dec_geo[k, i : i + 1, :]
            high = geo.astype(BF16).astype(F32)
            slab_dec[k, 4 + i : 5 + i, :] = high
            slab_dec[k, 8 + i : 9 + i, :] = geo - high
            slab_dec[k, 12 + i : 13 + i, :] = high
    total[...] = jnp.zeros(total.shape, F32)
    load(2).wait()
    self_part[...] = dot(own, w_node_self[...])
    load(1).wait()

    load(0).wait()
    load(6).wait()
    grid_part[...] = dot(grid[...], w_dec_grid[...])

    def pick_fine(slab):
        tail, sender, receiver = turn(slab)
        return jnp.concatenate([one_hot(sender, span), one_hot(receiver, nodes), tail], axis=1)

    settle(node_first, node_last, 0, edge_in)
    spread(spot)
    border = jnp.concatenate([edge_in[0], edge_in[1]], axis=0)
    border_proj = dot(border, w_send[...]).astype(BF16)
    table[0:BORDER, :] = border_proj[:BORDER]
    table[BORDER + nodes : span, :] = border_proj[BORDER:]

    def message_of(held):
        return normalize(dot(held, w_message[...])).astype(BF16)

    def add(place, message):
        total[...] += dot(one_hot_rows(place.astype(jnp.int32), nodes), message)

    loops = edges // CHUNK
    steps = [functools.partial(step_z, step) for step in range(1, line)]
    turns = [[] for _ in range(loops)]
    for number, step in enumerate(steps):
        turns[1 + number * (loops - 1) // len(steps)].append(step)

    hidden[...] = silu(dot(pick_fine(slab_fine[:, :CHUNK]), table[...])).astype(BF16)

    def fine(i, carry):
        for number, group_of in enumerate(turns):
            if group_of:

                @pl.when(i == number)
                def _():
                    for step in group_of:
                        step()

        at = pl.ds(pl.multiple_of(i * CHUNK, CHUNK), CHUNK)
        before = pl.ds(pl.multiple_of((i - 1) * CHUNK, CHUNK), CHUNK)
        held = dot(hidden[...], w_message[...])
        pre = dot(pick_fine(slab_fine[:, at]), table[...])
        add(slab_fine[1:2, before], normalize(held).astype(BF16))
        hidden[...] = silu(pre).astype(BF16)
        return carry

    lax.fori_loop(1, loops, fine, 0)
    step_y()
    add(slab_fine[1:2, edges - CHUNK :], message_of(hidden[...]))
    load(9).wait()
    grid_own[...] = dot(grid[...], w_grid_self[...])
    step_end()
    coarse_table[...] = dot(
        coarse[...].reshape(regions * COARSE, width), w_send[...]
    ).astype(BF16)
    reach = owners * COARSE
    for number in range(slots // group):
        slab = slab_long[:, number * group : (number + 1) * group]
        tail, sender, receiver = turn(slab)
        near = jnp.concatenate([one_hot(receiver, nodes), tail], axis=1)
        pre = dot(
            one_hot(sender, reach), coarse_table[number * reach : (number + 1) * reach, :]
        ) + dot(near, table[span:, :])
        add(slab[1:2, :], message_of(silu(pre).astype(BF16)))

    load(3).wait()
    load(4).wait()

    def refresh(aggregate, own_part, latent):
        hidden = silu(own_part + dot(aggregate.astype(BF16), w_node_agg[...])).astype(BF16)
        return (latent.astype(F32) + dot(hidden, w_node_out[...])).astype(BF16)

    def both(ref):
        return jnp.concatenate([ref[:BORDER, :], ref[nodes - BORDER :, :]], axis=0)

    ends = refresh(both(total), both(self_part), both(node))
    ends_out[0] = ends[:BORDER]
    ends_out[1] = ends[BORDER:]
    exchange(ends_out.at[0], ends_out.at[1], 1, ends_in)
    inner = slice(BORDER, nodes - BORDER)
    out_mesh[inner, :] = refresh(total[inner, :], self_part[inner, :], node[inner, :])
    out_mesh[:BORDER, :] = ends[:BORDER]
    out_mesh[nodes - BORDER :, :] = ends[BORDER:]
    load(5).wait()
    dec_table[BORDER : BORDER + nodes, :] = dot(out_mesh[...], w_dec_send[...]).astype(BF16)
    part = points // 2
    for number in range(2):
        span_of = slice(number * part, (number + 1) * part)
        tail, sender, _ = turn(jnp.concatenate([slab_dec[k, :, span_of] for k in range(3)], axis=1))
        picks[number, :, :span] = one_hot(sender, span)
        picks[number, :, span:] = tail
    for number in (7, 8, 10):
        load(number).wait()
    settle(ends_out.at[0], ends_out.at[1], 1, ends_in)
    border = jnp.concatenate([ends_in[0], ends_in[1]], axis=0)
    border_proj = dot(border, w_dec_send[...]).astype(BF16)
    dec_table[0:BORDER, :] = border_proj[:BORDER]
    dec_table[BORDER + nodes : span, :] = border_proj[BORDER:]

    for number in range(2):
        at = pl.ds(number * part, part)
        grid_three = jnp.concatenate([grid_part[at, :]] * 3, axis=0)
        pre = dot(picks[number], dec_table[...]) + grid_three
        message = normalize(dot(silu(pre).astype(BF16), w_dec_final[...]))
        gathered = message[:part] + message[part : 2 * part] + message[2 * part :]
        state = silu(dot(gathered.astype(BF16), w_grid_agg[...]) + grid_own[at, :])
        fields = lax.dot_general(
            w_final[...],
            state.astype(BF16),
            (((1,), (1,)), ((), ())),
            preferred_element_type=F32,
        )
        out_fields[:, at] = fields.astype(BF16)


def hand_over(mesh_in, fields_in, mesh_out, fields_out, sems):
    copies = (
        pltpu.make_async_copy(mesh_in, mesh_out, sems.at[0]),
        pltpu.make_async_copy(fields_in, fields_out, sems.at[1]),
    )
    for copy in copies:
        copy.start()
    for copy in copies:
        copy.wait()


def body(
    node_latent,
    grid_latent,
    fine_edge_sender,
    short_recv,
    short_geo,
    long_send,
    long_recv,
    long_geo,
    dec_send,
    dec_geo,
    w_send,
    w_recv,
    w_edge_geo,
    w_message,
    w_node_self,
    w_node_agg,
    w_node_out,
    w_dec_send,
    w_dec_grid,
    w_dec_geo,
    decoding_link_final_matrix,
    w_grid_agg,
    w_grid_self,
    final_projection_matrix,
):
    regions = lax.axis_size("region")
    nodes, width = node_latent.shape
    points = grid_latent.shape[0]
    edges, slots = fine_edge_sender.shape[0], long_send.shape[0]
    line = regions // 4
    fields = final_projection_matrix.shape[0]
    span = nodes + 2 * BORDER
    square = pltpu.VMEM((width, width), BF16)
    vmem = pl.BlockSpec(memory_space=pltpu.VMEM)
    anywhere = pl.BlockSpec(memory_space=pl.ANY)
    dma = pltpu.SemaphoreType.DMA

    def lanes(array):
        return array.reshape(-1, LANES)

    results = pl.pallas_call(
        functools.partial(kernel, regions),
        out_shape=(
            jax.ShapeDtypeStruct((nodes, width), BF16),
            jax.ShapeDtypeStruct((fields, points), BF16),
        ),
        in_specs=[vmem, anywhere] + [vmem] * 12 + [anywhere] * 10,
        out_specs=(vmem, vmem),
        scratch_shapes=[pltpu.VMEM((points, width), BF16)]
        + [square] * 9
        + [
            pltpu.VMEM((fields, width), BF16),
            dma((11,)),
            pltpu.VMEM((2, BORDER, width), BF16),
            pltpu.VMEM((2, BORDER, width), BF16),
            pltpu.VMEM((2, BORDER, width), BF16),
            dma((2, 2)),
            dma((2, 2)),
            pltpu.VMEM((regions, COARSE, width), BF16),
            dma((2, line)),
            dma((2, line)),
            dma((line,)),
            dma((line,)),
            dma((2, line)),
            dma((2, line)),
            pltpu.VMEM((span + nodes + TAIL, width), BF16),
            pltpu.VMEM((regions * COARSE, width), BF16),
            pltpu.VMEM((span + TAIL, width), BF16),
            pltpu.VMEM((16, edges), F32),
            pltpu.VMEM((16, slots), F32),
            pltpu.VMEM((3, 16, points), F32),
            pltpu.VMEM((nodes, width), F32),
            pltpu.VMEM((nodes, width), F32),
            pltpu.VMEM((points, width), F32),
            pltpu.VMEM((points, width), F32),
            pltpu.VMEM((CHUNK, width), BF16),
            pltpu.VMEM((2, 3 * (points // 2), span + TAIL), BF16),
        ],
        compiler_params=pltpu.CompilerParams(
            collective_id=0, has_side_effects=True, vmem_limit_bytes=56 * 1024 * 1024
        ),
        name="graph_round",
    )(
        node_latent,
        grid_latent,
        lanes(fine_edge_sender),
        lanes(short_recv),
        short_geo,
        lanes(long_send),
        lanes(long_recv),
        long_geo,
        dec_send,
        jnp.transpose(dec_geo, (1, 0, 2)),
        w_send,
        w_recv,
        w_edge_geo,
        w_dec_geo,
        w_message,
        w_node_self,
        w_node_agg,
        w_node_out,
        w_dec_send,
        w_dec_grid,
        decoding_link_final_matrix,
        w_grid_agg,
        w_grid_self,
        final_projection_matrix,
    )
    return pl.pallas_call(
        hand_over,
        out_shape=tuple(jax.ShapeDtypeStruct(array.shape, array.dtype) for array in results),
        in_specs=[anywhere] * 2,
        out_specs=(vmem,) * 2,
        scratch_shapes=[dma((2,))],
        compiler_params=pltpu.CompilerParams(vmem_limit_bytes=56 * 1024 * 1024),
        name="hand_over",
    )(*results)


def solution(mesh):
    split = ("ens", "region")
    in_specs = (
        P(split, None),
        P(split, None),
        P(split),
        P(split),
        P(None, split),
        P(split),
        P(split),
        P(None, split),
        P(None, split),
        P(None, None, split),
    ) + (P(),) * 14
    out_specs = (P(split, None), P(None, split))
    return jax.shard_map(body, mesh=mesh, in_specs=in_specs, out_specs=out_specs, check_vma=False)
```
